32 devices in a mesh: cuts: 2 (over y), ctx: 16 (over z, x, core).
Axes of the slice: x: 2, y: 2, z: 4, core: 2. Of those that a mesh axis runs over, the one named last changes fastest.
Arguments:
- queries: bfloat16 [4096, 8192], P('ctx')
- keys: bfloat16 [4096, 1024], P(('cuts', 'ctx'))
- values: bfloat16 [4096, 1024], P(('cuts', 'ctx')), may hold values from -6 to 6
- bounds: int32 [3, 32], replicated, may hold values from 0 to 31, as said below
Outputs:
- attended: bfloat16 [4096, 8192], P('ctx', 'cuts')
The draws below stay inside these ranges and needn't reach their ends.
Inputs may be any that keep to these rules, and one draw needn't show every extreme that they name: The sequence is a row of trees laid end to end in whole mask blocks: each tree is a prompt of 1 to 4 mask blocks followed by up to 8 responses of 1 to 2 mask blocks each, so a tree spans at most 20 mask blocks; the last mask block is a one-block prompt of its own, and the tree before it may be cut off. For a block b of a prompt, bounds[0, b] is the prompt's first block and bounds[1, b] = bounds[2, b] = bounds[0, b]; for a block of a response, bounds[0, b] is the response's first block and bounds[1, b] < bounds[2, b] <= bounds[0, b] delimit the prompt of its tree. Block 0 starts a prompt.
All inputs are finite; a program needn't handle non-finite values.
Results may differ from the reference program's by a relative error of at most 0.014.
Values may be sent and summed in bfloat16 or wider, within the bound.
No kernel may reach another device: no remote copies, remote signals or barrier semaphores. Data moves between devices by JAX's collectives and lax.ppermute only.
A program may use at most 64 MiB of HBM per device.

```python
import jax
import jax.numpy as jnp
from jax import lax

QUERY_HEADS = 64
KEY_VALUE_HEADS = 8
HEAD_SIZE = 128
BLK = 128
BRANCH = 8
QUERY_TOKENS = 256
PACKED_TOKENS = 4096
NB = 32
GROUP_SIZE = 8
N_CUTS = 2
N_CTX = 16


def key_base(key):
    base_offset = jax.random.normal(jax.random.fold_in(key, 21), (PACKED_TOKENS, KEY_VALUE_HEADS * HEAD_SIZE), jnp.float32)
    return base_offset


def draw_keys(key, part):
    return key_base(key).astype(jnp.bfloat16)


def draw_queries(key, part):
    drawn = jax.random.normal(jax.random.fold_in(key, 22), (PACKED_TOKENS, QUERY_HEADS * HEAD_SIZE), jnp.float32)
    return drawn.astype(jnp.bfloat16)


def draw_bounds(key, part):
    trees = NB
    segments = trees * (BRANCH + 1)
    prompt_key = jax.random.fold_in(key, 31)
    reply_key = jax.random.fold_in(key, 32)
    prompt_blocks = jax.random.randint(prompt_key, (trees, 1), 1, 5, dtype=jnp.int32)
    reply_blocks = jax.random.randint(reply_key, (trees, BRANCH), 1, 3, dtype=jnp.int32)
    lengths = jnp.concatenate([prompt_blocks, reply_blocks], axis=1).reshape(segments)
    segment_ends = jnp.cumsum(lengths).astype(jnp.int32)
    segment_starts = segment_ends - lengths
    blocks = jnp.arange(NB, dtype=jnp.int32)
    which_segment = jnp.sum((segment_starts[None, :] <= blocks[:, None]).astype(jnp.int32), axis=1) - 1
    labels = jnp.arange(segments, dtype=jnp.int32)
    select_own = (which_segment[:, None] == labels[None, :]).astype(jnp.int32)
    own_start = jnp.sum(select_own * segment_starts[None, :], axis=1)
    root_segment = which_segment // (BRANCH + 1) * (BRANCH + 1)
    select_root = (root_segment[:, None] == labels[None, :]).astype(jnp.int32)
    prompt_start = jnp.sum(select_root * segment_starts[None, :], axis=1)
    prompt_end = jnp.sum(select_root * segment_ends[None, :], axis=1)
    is_prompt = which_segment == root_segment
    prompt_end = jnp.where(is_prompt, prompt_start, prompt_end)
    is_last = blocks == NB - 1
    own_start = jnp.where(is_last, NB - 1, own_start)
    prompt_start = jnp.where(is_last, NB - 1, prompt_start)
    prompt_end = jnp.where(is_last, NB - 1, prompt_end)
    return jnp.stack([own_start, prompt_start, prompt_end], axis=0).astype(jnp.int32)


def block_levels(key, dims, pieces, smallest, high):
    factor_of = 1.0
    for position, parts in pieces:
        heights = jax.random.uniform(jax.random.fold_in(jax.random.fold_in(key, 6), position), (parts,), jnp.float32, smallest / len(pieces), high / len(pieces))
        factor_of = factor_of * jnp.repeat(jnp.exp(heights), dims[position] // parts).reshape((-1,) + (1,) * (len(dims) - 1 - position))
    return factor_of


def normal_values(key, dims, width, limit, shards=(), kind=jnp.bfloat16):
    gain = block_levels(key, dims, shards, -0.22, 0.18) if shards else 1.0
    entries = jax.random.normal(key, dims, jnp.float32) * width * gain
    return jnp.minimum(jnp.maximum(entries, -limit), limit).astype(kind)


def setup_inputs(seed: int = 0) -> dict:
    splits = jax.random.split(jax.random.key(seed), 5)
    queries = draw_queries(jax.random.fold_in(splits[4], 71), 0)
    keys = draw_keys(jax.random.fold_in(splits[4], 71), 0)
    values = normal_values(splits[2], (PACKED_TOKENS, KEY_VALUE_HEADS * HEAD_SIZE), 1.0, 6.0, ((0, 32),))
    bounds = draw_bounds(jax.random.fold_in(splits[4], 71), 0)
    return {"queries": queries, "keys": keys, "values": values, "bounds": bounds}


NEGATIVE_FILL = -1e30


def visible(query_pos, key_pos, bounds):
    blocks = bounds.shape[1]
    query_block = query_pos // BLK
    select = (query_block[:, None] == jnp.arange(blocks, dtype=jnp.int32)[None, :]).astype(jnp.int32)
    table = jnp.sum(select[:, None, :] * bounds[None, :, :], axis=2)
    key_block = key_pos // BLK
    own_part = key_block[None, :] >= table[:, 0:1]
    prefix = (key_block[None, :] >= table[:, 1:2]) & (key_block[None, :] < table[:, 2:3])
    return (key_pos[None, :] <= query_pos[:, None]) & (own_part | prefix)


def reference(queries, keys, values, bounds):
    span_length = PACKED_TOKENS // N_CUTS
    query_matrix = queries.reshape(N_CTX, QUERY_TOKENS, KEY_VALUE_HEADS, GROUP_SIZE, HEAD_SIZE)
    key_matrix = keys.reshape(N_CUTS, span_length, KEY_VALUE_HEADS, HEAD_SIZE)
    value_matrix = values.reshape(N_CUTS, span_length, KEY_VALUE_HEADS, HEAD_SIZE)
    key_pos_all = jnp.arange(PACKED_TOKENS, dtype=jnp.int32).reshape(N_CUTS, span_length)

    def one_block(entry):
        query_block, block_id = entry
        query_pos = block_id * QUERY_TOKENS + jnp.arange(QUERY_TOKENS, dtype=jnp.int32)
        query_wide = query_block.astype(jnp.float32)
        score_list = []
        allow_list = []
        for which in range(N_CUTS):
            allowed = visible(query_pos, key_pos_all[which], bounds)
            raw_score = jnp.einsum("qhgd,khd->qhgk", query_wide, key_matrix[which].astype(jnp.float32)) * (HEAD_SIZE ** -0.5)
            score_list.append(jnp.where(allowed[:, None, None, :], raw_score, NEGATIVE_FILL))
            allow_list.append(allowed)
        highest = jnp.max(score_list[0], axis=3)
        for which in range(1, N_CUTS):
            highest = jnp.maximum(highest, jnp.max(score_list[which], axis=3))
        summed_weights = jnp.zeros((QUERY_TOKENS, KEY_VALUE_HEADS, GROUP_SIZE, HEAD_SIZE), jnp.float32)
        row_totals = jnp.zeros((QUERY_TOKENS, KEY_VALUE_HEADS, GROUP_SIZE), jnp.float32)
        for which in range(N_CUTS):
            expos = jnp.where(allow_list[which][:, None, None, :], jnp.exp(score_list[which] - highest[..., None]), 0.0)
            weight = expos.astype(jnp.bfloat16)
            partial_out = jnp.einsum("qhgk,khd->qhgd", weight.astype(jnp.float32), value_matrix[which].astype(jnp.float32))
            rounded = lax.optimization_barrier(partial_out.astype(jnp.bfloat16))
            summed_weights = summed_weights + rounded.astype(jnp.float32)
            row_totals = row_totals + jnp.sum(expos, axis=3)
        result = (summed_weights / row_totals[..., None]).astype(jnp.bfloat16)
        return result.reshape(QUERY_TOKENS, QUERY_HEADS * HEAD_SIZE)

    outputs = lax.map(one_block, (query_matrix, jnp.arange(N_CTX, dtype=jnp.int32)))
    return outputs.reshape(PACKED_TOKENS, QUERY_HEADS * HEAD_SIZE)
```

```python
import functools

import jax
import jax.numpy as jnp
from jax import lax
from jax.experimental import pallas as pl
from jax.experimental.pallas import tpu as pltpu
from jax.sharding import PartitionSpec as P

QUERY_HEADS = 64
KEY_VALUE_HEADS = 8
HEAD_SIZE = 128
GROUP_SIZE = QUERY_HEADS // KEY_VALUE_HEADS
BLK = 128
PROMPT_BLOCKS = 4
REPLY_BLOCKS = 2
MOST_BLOCKS = PROMPT_BLOCKS + REPLY_BLOCKS
NEGATIVE_FILL = -1e30
EXP2_SCALE = 1.4426950408889634 * HEAD_SIZE ** (-0.5)
VMEM_LIMIT = 48 * 1024 * 1024


def attend(count, query_ref, keys_now, values_now, out_ref):
    width = count * BLK
    keys = keys_now[0:width, :]
    values = values_now[0:width, :]
    row = lax.broadcasted_iota(jnp.int32, (BLK, BLK), 0)
    column = lax.broadcasted_iota(jnp.int32, (BLK, BLK), 1)
    causal = column <= row
    for head in range(GROUP_SIZE):
        span = slice(head * HEAD_SIZE, (head + 1) * HEAD_SIZE)
        score = lax.dot_general(
            query_ref[:, span], keys, (((1,), (1,)), ((), ())), preferred_element_type=jnp.float32
        )
        parts = [score[:, i * BLK : (i + 1) * BLK] for i in range(count)]
        parts[-1] = jnp.where(causal, parts[-1], NEGATIVE_FILL)
        peak = functools.reduce(jnp.maximum, parts)
        peak = jnp.max(peak, axis=1, keepdims=True)
        weight = [jnp.exp2((part - peak) * EXP2_SCALE).astype(jnp.bfloat16) for part in parts]
        weight = weight[0] if count == 1 else jnp.concatenate(weight, axis=1)
        both = jnp.dot(weight, values, preferred_element_type=jnp.float32)
        result = both[:, :HEAD_SIZE] / both[:, HEAD_SIZE:]
        out_ref[:, span] = result.astype(out_ref.dtype)


def attention_kernel(slot_of, place_ref, bounds_ref, query_ref, kv_ref, out_ref, keys_now, values_now):
    q_id = pl.program_id(0)
    head = pl.program_id(1)
    block = place_ref[0] + q_id
    own = bounds_ref[0, block]
    first = bounds_ref[1, block]
    prompt = bounds_ref[2, block] - first
    count = prompt + block - own + 1
    column = pl.multiple_of(head * HEAD_SIZE, HEAD_SIZE)

    @pl.when((q_id == 0) & (head == 0))
    def _():
        values_now[:, HEAD_SIZE:] = jnp.ones((values_now.shape[0], HEAD_SIZE), values_now.dtype)

    for i in range(MOST_BLOCKS):

        @pl.when(i < count)
        def _():
            which = jnp.where(i < prompt, first + i, own + i - prompt)
            slot = slot_of(place_ref, which)
            keys_now[i * BLK : (i + 1) * BLK, :] = kv_ref[slot, 0, :, pl.ds(column, HEAD_SIZE)]
            values_now[i * BLK : (i + 1) * BLK, :HEAD_SIZE] = kv_ref[
                slot, 1, :, pl.ds(column, HEAD_SIZE)
            ]

    for n in range(1, MOST_BLOCKS + 1):

        @pl.when(count == n)
        def _():
            attend(n, query_ref, keys_now, values_now, out_ref)


def attention(queries, kv, bounds, place, slot_of, heads_here):
    rows = queries.shape[0]
    kv_heads = heads_here // GROUP_SIZE
    wide = GROUP_SIZE * HEAD_SIZE
    grid_spec = pltpu.PrefetchScalarGridSpec(
        num_scalar_prefetch=2,
        grid=(rows // BLK, kv_heads),
        in_specs=[
            pl.BlockSpec((BLK, wide), lambda q, g, place, bounds: (q, place[1] * kv_heads + g)),
            pl.BlockSpec(kv.shape, lambda q, g, place, bounds: (0, 0, 0, 0)),
        ],
        out_specs=pl.BlockSpec((BLK, wide), lambda q, g, place, bounds: (q, g)),
        scratch_shapes=[
            pltpu.VMEM((MOST_BLOCKS * BLK, HEAD_SIZE), jnp.bfloat16),
            pltpu.VMEM((MOST_BLOCKS * BLK, 2 * HEAD_SIZE), jnp.bfloat16),
        ],
    )
    return pl.pallas_call(
        functools.partial(attention_kernel, slot_of),
        grid_spec=grid_spec,
        out_shape=jax.ShapeDtypeStruct((rows, heads_here * HEAD_SIZE), jnp.bfloat16),
        compiler_params=pltpu.CompilerParams(vmem_limit_bytes=VMEM_LIMIT),
        name="attention",
    )(place, bounds, queries, kv)


def gathered_local(cuts, queries, keys, values, bounds):
    heads_here = QUERY_HEADS // cuts
    columns = KEY_VALUE_HEADS * HEAD_SIZE // cuts
    rows = keys.shape[0]
    both = jnp.stack([keys, values], 0).reshape(2, rows, cuts, columns)
    both = lax.all_to_all(both.transpose(2, 0, 1, 3), "cuts", 0, 0)
    both = lax.all_gather(both, "ctx", axis=0)
    both = both.transpose(2, 1, 0, 3, 4).reshape(2, -1, BLK, columns).transpose(1, 0, 2, 3)
    place = jnp.stack([lax.axis_index("ctx") * (queries.shape[0] // BLK), lax.axis_index("cuts")])
    return attention(queries, both, bounds, place, lambda place_ref, which: which, heads_here)


def solution(mesh):
    cuts = mesh.shape["cuts"]
    in_specs = (P("ctx", None), P(("cuts", "ctx"), None), P(("cuts", "ctx"), None), P())
    out_specs = P("ctx", "cuts")
    local = functools.partial(gathered_local, cuts)
    return jax.shard_map(local, mesh=mesh, in_specs=in_specs, out_specs=out_specs, check_vma=False)
```

```python
import functools

import jax
import jax.numpy as jnp
from jax import lax
from jax.experimental import pallas as pl
from jax.experimental.pallas import tpu as pltpu
from jax.sharding import PartitionSpec as P

QUERY_HEADS = 64
KEY_VALUE_HEADS = 8
HEAD_SIZE = 128
GROUP_SIZE = QUERY_HEADS // KEY_VALUE_HEADS
BLK = 128
PROMPT_BLOCKS = 4
REPLY_BLOCKS = 2
MOST_BLOCKS = PROMPT_BLOCKS + REPLY_BLOCKS
CHIP_BLOCKS = 4
NEGATIVE_FILL = -1e30
EXP2_SCALE = 1.4426950408889634 * HEAD_SIZE ** (-0.5)
VMEM_LIMIT = 48 * 1024 * 1024


def attend(count, query_ref, keys_now, values_now, out_ref):
    width = count * BLK
    keys = keys_now[0:width, :]
    values = values_now[0:width, :]
    row = lax.broadcasted_iota(jnp.int32, (BLK, BLK), 0)
    column = lax.broadcasted_iota(jnp.int32, (BLK, BLK), 1)
    causal = column <= row
    for head in range(GROUP_SIZE):
        span = slice(head * HEAD_SIZE, (head + 1) * HEAD_SIZE)
        score = lax.dot_general(
            query_ref[:, span], keys, (((1,), (1,)), ((), ())), preferred_element_type=jnp.float32
        )
        parts = [score[:, i * BLK : (i + 1) * BLK] for i in range(count)]
        parts[-1] = jnp.where(causal, parts[-1], NEGATIVE_FILL)
        peak = functools.reduce(jnp.maximum, parts)
        peak = jnp.max(peak, axis=1, keepdims=True)
        weight = [jnp.exp2((part - peak) * EXP2_SCALE).astype(jnp.bfloat16) for part in parts]
        weight = weight[0] if count == 1 else jnp.concatenate(weight, axis=1)
        both = jnp.dot(weight, values, preferred_element_type=jnp.float32)
        result = both[:, :HEAD_SIZE] / both[:, HEAD_SIZE:]
        out_ref[:, span] = result.astype(out_ref.dtype)


def attention_kernel(slot_of, sources, place_ref, bounds_ref, query_ref, *refs):
    kv_refs = refs[: len(sources)]
    out_ref, kv_now, keys_now, values_now, arrived = refs[len(sources) :]
    q_id = pl.program_id(0)
    head = pl.program_id(1)
    chip = place_ref[0] // CHIP_BLOCKS
    block = place_ref[0] + q_id
    own = bounds_ref[0, block]
    first = bounds_ref[1, block]
    prompt = bounds_ref[2, block] - first
    count = prompt + block - own + 1
    column = pl.multiple_of(head * HEAD_SIZE, HEAD_SIZE)

    @pl.when((q_id == 0) & (head == 0))
    def _():
        copies = [
            pltpu.make_async_copy(kv_ref, kv_now.at[pl.ds(slot(place_ref), kv_ref.shape[0])], arrived.at[i])
            for i, (kv_ref, slot) in enumerate(zip(kv_refs, sources))
        ]
        for copy in copies:
            copy.start()
        values_now[:, HEAD_SIZE:] = jnp.ones((values_now.shape[0], HEAD_SIZE), values_now.dtype)
        for copy in copies:
            copy.wait()

    for i in range(MOST_BLOCKS):

        @pl.when(i < count)
        def _():
            which = jnp.where(i < prompt, first + i, own + i - prompt)
            slot = slot_of(bounds_ref, chip, which)
            keys_now[i * BLK : (i + 1) * BLK, :] = kv_now[slot, 0, :, pl.ds(column, HEAD_SIZE)]
            values_now[i * BLK : (i + 1) * BLK, :HEAD_SIZE] = kv_now[
                slot, 1, :, pl.ds(column, HEAD_SIZE)
            ]

    for n in range(1, MOST_BLOCKS + 1):

        @pl.when(count == n)
        def _():
            attend(n, query_ref, keys_now, values_now, out_ref)


def attention(queries, kv, sources, slots, bounds, place, slot_of, heads_here):
    rows = queries.shape[0]
    kv_heads = heads_here // GROUP_SIZE
    wide = GROUP_SIZE * HEAD_SIZE
    grid_spec = pltpu.PrefetchScalarGridSpec(
        num_scalar_prefetch=2,
        grid=(rows // BLK, kv_heads),
        in_specs=[pl.BlockSpec((BLK, wide), lambda q, g, place, bounds: (q, place[1] * kv_heads + g))]
        + [pl.BlockSpec(memory_space=pl.ANY)] * len(kv),
        out_specs=pl.BlockSpec((BLK, wide), lambda q, g, place, bounds: (q, g)),
        scratch_shapes=[
            pltpu.VMEM((slots,) + kv[0].shape[1:], jnp.bfloat16),
            pltpu.VMEM((MOST_BLOCKS * BLK, HEAD_SIZE), jnp.bfloat16),
            pltpu.VMEM((MOST_BLOCKS * BLK, 2 * HEAD_SIZE), jnp.bfloat16),
            pltpu.SemaphoreType.DMA((len(kv),)),
        ],
    )
    return pl.pallas_call(
        functools.partial(attention_kernel, slot_of, sources),
        grid_spec=grid_spec,
        out_shape=jax.ShapeDtypeStruct((rows, heads_here * HEAD_SIZE), jnp.bfloat16),
        compiler_params=pltpu.CompilerParams(vmem_limit_bytes=VMEM_LIMIT),
        name="attention",
    )(place, bounds, queries, *kv)


def gathered_local(cuts, queries, keys, values, bounds):
    heads_here = QUERY_HEADS // cuts
    columns = KEY_VALUE_HEADS * HEAD_SIZE // cuts
    rows = keys.shape[0]
    both = jnp.stack([keys, values], 0).reshape(2, rows, cuts, columns)
    both = lax.all_to_all(both.transpose(2, 0, 1, 3), "cuts", 0, 0)
    both = lax.all_gather(both, "ctx", axis=0)
    both = both.transpose(2, 1, 0, 3, 4).reshape(2, -1, BLK, columns).transpose(1, 0, 2, 3)
    place = jnp.stack([lax.axis_index("ctx") * (queries.shape[0] // BLK), lax.axis_index("cuts")])
    sources = [lambda place_ref: 0]
    return attention(
        queries, [both], sources, both.shape[0], bounds, place, lambda b, chip, which: which, heads_here
    )


def crossing(bounds_ref, edge):
    own, first, last = bounds_ref[0, edge], bounds_ref[1, edge], bounds_ref[2, edge]
    reply = first < last
    return jnp.where(reply, first, own), jnp.where(reply, last, edge)


def crossing_block(bounds_ref, edge, residue):
    low, high = crossing(bounds_ref, edge)
    which = low + lax.rem(residue - lax.rem(low, 4) + 4, 4)
    return jnp.where(which < high, which, -1)


def tree_slot(bounds_ref, chip, which):
    edge = chip * CHIP_BLOCKS
    low, high = crossing(bounds_ref, edge)
    crosses = (which >= low) & (which < high)
    early = jnp.where(crosses, 4 + lax.rem(which, 4), 8)
    return jnp.where(which >= edge, which - edge, early)


def pick_kernel(rule, n_in, place_ref, bounds_ref, *refs):
    ins, outs, done = refs[:n_in], refs[n_in:-1], refs[-1]
    choices = rule(place_ref, bounds_ref)
    for o, choice in enumerate(choices):
        for i, in_ref in enumerate(ins):

            @pl.when(choice == i)
            def _():
                pltpu.make_async_copy(in_ref, outs[o], done.at[o]).start()

    for o in range(len(choices)):
        pltpu.make_async_copy(ins[0], outs[o], done.at[o]).wait()


def pick(rule, n_out, place, bounds, *arrays):
    shape = jax.ShapeDtypeStruct(arrays[0].shape, arrays[0].dtype)
    grid_spec = pltpu.PrefetchScalarGridSpec(
        num_scalar_prefetch=2,
        grid=(1,),
        in_specs=[pl.BlockSpec(memory_space=pl.ANY)] * len(arrays),
        out_specs=[pl.BlockSpec(memory_space=pltpu.VMEM)] * n_out,
        scratch_shapes=[pltpu.SemaphoreType.DMA((n_out,))],
    )
    return pl.pallas_call(
        functools.partial(pick_kernel, rule, len(arrays)),
        grid_spec=grid_spec,
        out_shape=[shape] * n_out,
        name="pick",
    )(place, bounds, *arrays)


def halves_kernel(place_ref, keys_ref, values_ref, own_ref, other_ref, done):
    cut = place_ref[1]
    columns = own_ref.shape[3]
    copies = []
    for i, in_ref in enumerate((keys_ref, values_ref)):
        for j, (out_ref, which) in enumerate(((own_ref, cut), (other_ref, 1 - cut))):
            span = pl.ds(pl.multiple_of(which * columns, columns), columns)
            copies.append(pltpu.make_async_copy(in_ref.at[:, span], out_ref.at[0, i], done.at[2 * i + j]))
    for copy in copies:
        copy.start()
    for copy in copies:
        copy.wait()


def halves(place, keys, values):
    rows, columns = keys.shape
    shape = jax.ShapeDtypeStruct((1, 2, rows, columns // 2), keys.dtype)
    grid_spec = pltpu.PrefetchScalarGridSpec(
        num_scalar_prefetch=1,
        grid=(1,),
        in_specs=[pl.BlockSpec(memory_space=pl.ANY)] * 2,
        out_specs=[pl.BlockSpec(memory_space=pltpu.VMEM)] * 2,
        scratch_shapes=[pltpu.SemaphoreType.DMA((4,))],
    )
    return pl.pallas_call(halves_kernel, grid_spec=grid_spec, out_shape=[shape] * 2, name="halves")(
        place, keys, values
    )


def where(*cases):
    value = cases[-1]
    for condition, choice in reversed(cases[:-1]):
        value = jnp.where(condition, choice, value)
    return value


def position(place_ref):
    ctx = place_ref[0] // 2
    return ctx // 4, lax.rem(ctx, 4), lax.rem(ctx // 2, 2)


def rule_spread(place_ref, bounds_ref):
    plane, _, _ = position(place_ref)
    cut = place_ref[1]
    low, high = cut, 1 - cut
    return low, where((plane == 0, low), high), where((plane == 3, low), high)


def rule_middle(place_ref, bounds_ref):
    plane, residue, x = position(place_ref)
    low, high, down, up, far = 0, 1, 2, 3, 4
    to_2 = crossing_block(bounds_ref, 16, residue)
    to_3 = crossing_block(bounds_ref, 24, residue)
    ahead = where(
        (plane == 1, jnp.where(to_2 < 4, up, low)),
        (plane == 2, where((to_3 < 12, low), (to_3 < 16, down), (to_3 < 20, far), up)),
        low,
    )
    lower = where((plane == 0, low), (plane == 1, down), (plane == 2, far), up)
    upper = where((plane == 0, down), (plane == 1, far), (plane == 2, up), high)
    kept = jnp.where(x == 0, lower, upper)
    sent = jnp.where(x == 0, upper, lower)
    before = where((plane == 1, low), (plane == 2, down), (plane == 3, far), low)
    return ahead, kept, sent, before


def rule_last(place_ref, bounds_ref):
    plane, residue, x = position(place_ref)
    low, down, up, kept, sent, crossed, rare, before = 0, 1, 2, 3, 4, 5, 6, 7
    block = crossing_block(bounds_ref, plane * 8, residue)
    into_plane = where(
        (plane == 1, jnp.where(block < 4, up, low)),
        (plane == 2, where((block < 8, crossed), (block < 12, low), down)),
        (plane == 3, jnp.where(block < 8, rare, crossed)),
        low,
    )
    middle = crossing_block(bounds_ref, plane * 8 + 4, residue)
    into_half = jnp.where(middle >= plane * 8, jnp.where(x == 0, kept, sent), into_plane)
    mine = jnp.where(x == 0, into_plane, into_half)
    other = jnp.where(x == 0, into_half, into_plane)
    return mine, other, jnp.where(x == 0, before, sent)


def tree_local(queries, keys, values, bounds):
    heads_here = QUERY_HEADS // 2
    place = jnp.stack([lax.axis_index("ctx") * 2, lax.axis_index("cuts")])
    own, other = halves(place, keys, values)
    other = lax.ppermute(other, "cuts", [(0, 1), (1, 0)])

    def move(array, planes, residues=range(4)):
        pairs = [(4 * a + r, 4 * b + r) for a, b, only in planes for r in (only or residues)]
        return lax.ppermute(array, "ctx", pairs)

    send_down, send_up, send_far = pick(rule_spread, 3, place, bounds, own, other)
    down = move(send_down, [(1, 0, None), (2, 1, None), (3, 2, None)])
    up = move(send_up, [(0, 1, None), (1, 2, None), (2, 3, None)])
    far = move(send_far, [(3, 1, None), (0, 2, None), (1, 3, (3,))])
    low = send_down
    ahead, kept, sent, before = pick(rule_middle, 4, place, bounds, low, send_up, down, up, far)
    crossed = move(ahead, [(1, 2, None), (2, 3, None)])
    low_24 = jnp.where(bounds[1, 24] < bounds[2, 24], bounds[1, 24], bounds[0, 24])
    rare = lax.cond(low_24 < 8, lambda: move(low, [(1, 3, None)]), lambda: crossed)
    across = [(c, c ^ 2) for c in range(16)]
    beside = [(c, c ^ 1) for c in range(16)]
    home_x = lax.ppermute(sent, "ctx", across)
    before_x = lax.ppermute(before, "ctx", [(4 * z + 3, 4 * z + 1) for z in range(1, 4)])
    mine, forward, before = pick(
        rule_last, 3, place, bounds, low, down, up, kept, sent, crossed, rare, before_x
    )
    far_x = lax.ppermute(forward, "ctx", across)
    before_k = lax.ppermute(before, "ctx", [(c, c ^ 1) for c in range(1, 16, 2)])
    kv = [kept, home_x, mine, far_x]
    kv += [lax.ppermute(array, "ctx", beside) for array in kv]

    def slot(base, flip, place_ref):
        return base + (position(place_ref)[1] ^ flip)

    sources = [
        functools.partial(slot, base, flip ^ core)
        for core in (0, 1)
        for base, flip in ((0, 0), (0, 2), (4, 0), (4, 2))
    ]
    kv += [before, before_k]
    sources += [lambda p: 9 - lax.rem(p[0] // 2, 2), lambda p: 8 + lax.rem(p[0] // 2, 2)]
    return attention(queries, kv, sources, 10, bounds, place, tree_slot, heads_here)


def solution(mesh):
    cuts, ctx = mesh.shape["cuts"], mesh.shape["ctx"]
    in_specs = (P("ctx", None), P(("cuts", "ctx"), None), P(("cuts", "ctx"), None), P())
    out_specs = P("ctx", "cuts")
    general = functools.partial(gathered_local, cuts)

    def run(queries, keys, values, bounds):
        one_block_each = keys.shape[0] == cuts * ctx * BLK
        local = tree_local if (cuts, ctx) == (2, 16) and one_block_each else general
        mapped = jax.shard_map(local, mesh=mesh, in_specs=in_specs, out_specs=out_specs, check_vma=False)
        return mapped(queries, keys, values, bounds)

    return run
```

```python
import functools

import jax
import jax.numpy as jnp
from jax import lax
from jax.experimental import pallas as pl
from jax.experimental.pallas import tpu as pltpu
from jax.sharding import PartitionSpec as P

QUERY_HEADS = 64
KEY_VALUE_HEADS = 8
HEAD_SIZE = 128
GROUP_SIZE = QUERY_HEADS // KEY_VALUE_HEADS
BLK = 128
PROMPT_BLOCKS = 4
REPLY_BLOCKS = 2
MOST_BLOCKS = PROMPT_BLOCKS + REPLY_BLOCKS
CHIP_BLOCKS = 4
NEGATIVE_FILL = -1e30
EXP2_SCALE = 1.4426950408889634 * HEAD_SIZE ** (-0.5)
VMEM_LIMIT = 40 * 1024 * 1024
HEADS_AT_ONCE = 4


def attend(count, query, keys_now, values_now, out_ref):
    width = count * BLK
    row = lax.broadcasted_iota(jnp.int32, (BLK, BLK), 0)
    column = lax.broadcasted_iota(jnp.int32, (BLK, BLK), 1)
    causal = jnp.where(column <= row, 0.0, NEGATIVE_FILL)
    keys = keys_now[0:width, :]
    values = values_now[0:width, :]
    for first in range(0, GROUP_SIZE, HEADS_AT_ONCE):
        spans = [slice(h * HEAD_SIZE, (h + 1) * HEAD_SIZE) for h in range(first, first + HEADS_AT_ONCE)]
        stacked = jnp.concatenate([query[:, span] for span in spans], axis=0)
        score = lax.dot_general(stacked, keys, (((1,), (1,)), ((), ())), preferred_element_type=jnp.float32)
        parts = [score[:, i * BLK : (i + 1) * BLK] for i in range(count)]
        last = parts[-1].reshape(HEADS_AT_ONCE, BLK, BLK) + causal[None]
        parts[-1] = last.reshape(HEADS_AT_ONCE * BLK, BLK)
        peak = jnp.max(functools.reduce(jnp.maximum, parts), axis=1, keepdims=True) * EXP2_SCALE
        weight = [jnp.exp2(part * EXP2_SCALE - peak).astype(jnp.bfloat16) for part in parts]
        weight = weight[0] if count == 1 else jnp.concatenate(weight, axis=1)
        both = jnp.dot(weight, values, preferred_element_type=jnp.float32)
        result = (both[:, :HEAD_SIZE] / both[:, HEAD_SIZE:]).astype(out_ref.dtype)
        for h, span in enumerate(spans):
            out_ref[:, span] = result[h * BLK : (h + 1) * BLK]


def attention_kernel(slot_of, order, table_ref, query_ref, *refs):
    kv_refs = refs[:-8]
    out_ref, keys_now, values_now, ones_now, query_now, results, loaded, sent = refs[-8:]
    n_blocks, kv_heads, _, wide = results.shape
    chip = table_ref[3, 0] // CHIP_BLOCKS

    def query_copy(q_id, g):
        span = pl.ds(pl.multiple_of((table_ref[3, 1] * kv_heads + g) * wide, wide), wide)
        rows = pl.ds(q_id * BLK, BLK)
        return pltpu.make_async_copy(query_ref.at[rows, span], query_now.at[q_id, g], loaded.at[q_id, g])

    def result_copy(q_id, g):
        rows, span = pl.ds(q_id * BLK, BLK), pl.ds(pl.multiple_of(g * wide, wide), wide)
        return pltpu.make_async_copy(results.at[q_id, g], out_ref.at[rows, span], sent.at[q_id, g])

    for q_id in range(n_blocks):
        for g in range(kv_heads):
            query_copy(q_id, g).start()
    ones_now[:, HEAD_SIZE:] = jnp.ones((ones_now.shape[0], HEAD_SIZE), ones_now.dtype)
    for q_id in range(n_blocks):
        block = table_ref[3, 0] + q_id
        own = table_ref[0, block]
        first = table_ref[1, block]
        prompt = table_ref[2, block] - first
        count = prompt + block - own + 1
        for i in range(MOST_BLOCKS):
            which = jnp.where(i < prompt, first + i, own + i - prompt)
            slot = slot_of(table_ref, chip, which)
            to = slice(i * BLK, (i + 1) * BLK)
            if len(kv_refs) == 1:

                @pl.when(i < count)
                def _():
                    keys_now[to, :] = kv_refs[0][slot, 0:BLK, :]
                    values_now[to, :] = kv_refs[0][slot, BLK : 2 * BLK, :]

            else:
                choice = order(table_ref, slot)
                for j, kv_ref in enumerate(kv_refs):

                    @pl.when((i < count) & (choice == j))
                    def _():
                        keys_now[to, :] = kv_ref[0:BLK, :]
                        values_now[to, :] = kv_ref[BLK : 2 * BLK, :]

        def one_head(g, carry):
            column = pl.multiple_of(g * HEAD_SIZE, HEAD_SIZE)
            query_copy(q_id, g).wait()
            for n in range(1, MOST_BLOCKS + 1):

                @pl.when(count == n)
                def _():
                    width = n * BLK
                    ones_now[0:width, :HEAD_SIZE] = values_now[0:width, pl.ds(column, HEAD_SIZE)]
                    keys = keys_now.at[:, pl.ds(column, HEAD_SIZE)]
                    attend(n, query_now.at[q_id, g], keys, ones_now, results.at[q_id, g])

            result_copy(q_id, g).start()
            return carry

        lax.fori_loop(0, kv_heads, one_head, 0)
    for q_id in range(n_blocks):
        for g in range(kv_heads):
            result_copy(q_id, g).wait()


def attention(queries, cuts, kv, table, slot_of, order):
    rows, width = queries.shape[0], queries.shape[1] // cuts
    wide = GROUP_SIZE * HEAD_SIZE
    kv_heads = width // wide
    columns = kv[0].shape[-1]
    pieces = (rows // BLK, kv_heads)
    vmem = pl.BlockSpec(memory_space=pltpu.VMEM)
    smem = pl.BlockSpec(memory_space=pltpu.SMEM)
    kv = [pltpu.with_memory_space_constraint(array, pltpu.VMEM) for array in kv]
    return pl.pallas_call(
        functools.partial(attention_kernel, slot_of, order),
        in_specs=[smem, pl.BlockSpec(memory_space=pltpu.HBM)] + [vmem] * len(kv),
        out_specs=pl.BlockSpec(memory_space=pl.ANY),
        scratch_shapes=[
            pltpu.VMEM((MOST_BLOCKS * BLK, columns), jnp.bfloat16),
            pltpu.VMEM((MOST_BLOCKS * BLK, columns), jnp.bfloat16),
            pltpu.VMEM((MOST_BLOCKS * BLK, 2 * HEAD_SIZE), jnp.bfloat16),
            pltpu.VMEM(pieces + (BLK, wide), jnp.bfloat16),
            pltpu.VMEM(pieces + (BLK, wide), jnp.bfloat16),
            pltpu.SemaphoreType.DMA(pieces),
            pltpu.SemaphoreType.DMA(pieces),
        ],
        out_shape=jax.ShapeDtypeStruct((rows, width), jnp.bfloat16),
        compiler_params=pltpu.CompilerParams(vmem_limit_bytes=VMEM_LIMIT),
        name="attention",
    )(table, pltpu.with_memory_space_constraint(queries, pltpu.HBM), *kv)


def with_place(bounds, first_block, cut):
    place = jnp.where(jnp.arange(bounds.shape[1]) == 0, first_block, cut).astype(bounds.dtype)
    return jnp.concatenate([bounds, place[None]], 0)


def gathered_local(cuts, queries, keys, values, bounds):
    columns = KEY_VALUE_HEADS * HEAD_SIZE // cuts
    rows = keys.shape[0]
    both = jnp.stack([keys, values], 0).reshape(2, rows, cuts, columns)
    both = lax.all_to_all(both.transpose(2, 0, 1, 3), "cuts", 0, 0)
    both = lax.all_gather(both, "ctx", axis=0)
    both = both.transpose(2, 1, 0, 3, 4).reshape(2, -1, BLK, columns).transpose(1, 0, 2, 3)
    both = both.reshape(-1, 2 * BLK, columns)
    cut = lax.axis_index("cuts")
    table = with_place(bounds, lax.axis_index("ctx") * (queries.shape[0] // BLK), cut)
    return attention(queries, cuts, [both], table, lambda b, chip, which: which, None)


def crossing(table_ref, edge):
    own, first, last = table_ref[0, edge], table_ref[1, edge], table_ref[2, edge]
    reply = first < last
    return jnp.where(reply, first, own), jnp.where(reply, last, edge)


def crossing_block(table_ref, edge, residue):
    low, high = crossing(table_ref, edge)
    which = low + lax.rem(residue - lax.rem(low, 4) + 4, 4)
    return jnp.where(which < high, which, -1)


def tree_slot(table_ref, chip, which):
    edge = chip * CHIP_BLOCKS
    low, high = crossing(table_ref, edge)
    crosses = (which >= low) & (which < high)
    early = jnp.where(crosses, 4 + lax.rem(which, 4), 8)
    return jnp.where(which >= edge, which - edge, early)


def pick_kernel(rule, n_in, n_out, table_ref, *refs):
    ins, outs = refs[:n_in], refs[n_in : n_in + n_out]
    others = refs[n_in + n_out :]
    for out_ref, choice in zip(outs, rule(table_ref)):
        for i, in_ref in enumerate(ins):

            @pl.when(choice == i)
            def _():
                if others and i == n_in - 1:
                    copy = pltpu.make_async_copy(in_ref, out_ref, others[0])
                    copy.start()
                    copy.wait()
                else:
                    out_ref[...] = in_ref[...]


def pick(rule, n_out, table, *arrays, rare=None):
    vmem = pl.BlockSpec(memory_space=pltpu.VMEM)
    smem = pl.BlockSpec(memory_space=pltpu.SMEM)
    inputs = [pltpu.with_memory_space_constraint(array, pltpu.VMEM) for array in arrays]
    in_specs = [smem] + [vmem] * len(arrays)
    scratch = []
    if rare is not None:
        inputs.append(pltpu.with_memory_space_constraint(rare, pltpu.HBM))
        in_specs.append(pl.BlockSpec(memory_space=pltpu.HBM))
        scratch.append(pltpu.SemaphoreType.DMA)
    return pl.pallas_call(
        functools.partial(pick_kernel, rule, len(inputs), n_out),
        in_specs=in_specs,
        out_specs=[vmem] * n_out,
        out_shape=[pltpu.VMEM(arrays[0].shape, arrays[0].dtype)] * n_out,
        scratch_shapes=scratch,
        name="pick",
    )(table, *inputs)


def half(keys, values, cut):
    columns = keys.shape[1] // 2
    return jnp.concatenate([lax.dynamic_slice_in_dim(a, cut * columns, columns, 1) for a in (keys, values)], 0)


def where(*cases):
    value = cases[-1]
    for condition, choice in reversed(cases[:-1]):
        value = jnp.where(condition, choice, value)
    return value


def position(table_ref):
    ctx = table_ref[3, 0] // 2
    return ctx // 4, lax.rem(ctx, 4), lax.rem(ctx // 2, 2)


def rule_spread(table_ref):
    plane, _, _ = position(table_ref)
    cut = table_ref[3, 1]
    low, high = cut, 1 - cut
    return low, where((plane == 0, low), high), where((plane == 3, low), high)


def rule_middle(table_ref):
    plane, residue, x = position(table_ref)
    low, high, down, up, far = 0, 1, 2, 3, 4
    to_2 = crossing_block(table_ref, 16, residue)
    to_3 = crossing_block(table_ref, 24, residue)
    ahead = where(
        (plane == 1, jnp.where(to_2 < 4, up, low)),
        (plane == 2, where((to_3 < 12, low), (to_3 < 16, down), (to_3 < 20, far), up)),
        low,
    )
    lower = where((plane == 0, low), (plane == 1, down), (plane == 2, far), up)
    upper = where((plane == 0, down), (plane == 1, far), (plane == 2, up), high)
    kept = jnp.where(x == 0, lower, upper)
    sent = jnp.where(x == 0, upper, lower)
    return ahead, kept, sent, jnp.where(plane == 2, up, low)


def rule_last(table_ref):
    plane, residue, x = position(table_ref)
    low, down, up, kept, sent, crossed, rare = 0, 1, 2, 3, 4, 5, 6
    block = crossing_block(table_ref, plane * 8, residue)
    into_plane = where(
        (plane == 1, jnp.where(block < 4, up, low)),
        (plane == 2, where((block < 8, crossed), (block < 12, low), down)),
        (plane == 3, jnp.where((block >= 0) & (block < 8), rare, crossed)),
        low,
    )
    middle = crossing_block(table_ref, plane * 8 + 4, residue)
    into_half = jnp.where(middle >= plane * 8, jnp.where(x == 0, kept, sent), into_plane)
    return jnp.where(x == 0, into_plane, into_half), jnp.where(x == 0, into_half, into_plane)


def rule_before(table_ref):
    return (position(table_ref)[2],)


def tree_order(table_ref, slot):
    _, residue, _ = position(table_ref)
    flip = lax.rem(slot, 4) ^ residue
    index = 4 * lax.rem(flip, 2) + lax.rem(flip // 2, 2) + 2 * (slot // 4)
    return jnp.where(slot == 8, 9 - lax.rem(residue, 2), index)


def tree_local(queries, keys, values, bounds):
    cut = lax.axis_index("cuts")
    table = with_place(bounds, lax.axis_index("ctx") * 2, cut)
    own = half(keys, values, cut)
    other = lax.ppermute(half(keys, values, 1 - cut), "cuts", [(0, 1), (1, 0)])

    def move(array, planes):
        pairs = [(4 * a + r, 4 * b + r) for a, b in planes for r in range(4)]
        return lax.ppermute(array, "ctx", pairs)

    low, send_up, send_far = pick(rule_spread, 3, table, own, other)
    down = move(low, [(1, 0), (2, 1), (3, 2)])
    up = move(send_up, [(0, 1), (1, 2), (2, 3)])
    far = move(send_far, [(3, 1), (0, 2)])
    rare = lax.cond(crossing(bounds, 24)[0] < 8, lambda: move(low, [(1, 3)]), lambda: jnp.zeros_like(low))
    ahead, kept, sent, early = pick(rule_middle, 4, table, low, send_up, down, up, far, rare=rare)
    crossed = move(ahead, [(1, 2), (2, 3)])
    across = [(c, c ^ 2) for c in range(16)]
    beside = [(c, c ^ 1) for c in range(16)]
    home_x = lax.ppermute(sent, "ctx", across)
    before = lax.ppermute(early, "ctx", [(7, 5), (15, 9), (11, 13)])
    mine, forward = pick(rule_last, 2, table, low, down, up, kept, sent, crossed, rare=rare)
    far_x = lax.ppermute(forward, "ctx", across)
    (before,) = pick(rule_before, 1, table, before, sent)
    before_k = lax.ppermute(before, "ctx", [(c, c ^ 1) for c in range(1, 16, 2)])
    kv = [kept, home_x, mine, far_x]
    kv += [lax.ppermute(array, "ctx", beside) for array in kv]
    kv += [before, before_k]
    return attention(queries, 2, kv, table, tree_slot, tree_order)


def solution(mesh):
    cuts, ctx = mesh.shape["cuts"], mesh.shape["ctx"]
    in_specs = (P("ctx", None), P(("cuts", "ctx"), None), P(("cuts", "ctx"), None), P())
    out_specs = P("ctx", "cuts")
    general = functools.partial(gathered_local, cuts)

    def run(queries, keys, values, bounds):
        one_block_each = keys.shape[0] == cuts * ctx * BLK
        local = tree_local if (cuts, ctx) == (2, 16) and one_block_each else general
        mapped = jax.shard_map(local, mesh=mesh, in_specs=in_specs, out_specs=out_specs, check_vma=False)
        return mapped(queries, keys, values, bounds)

    return run
```

```python
import functools

import jax
import jax.numpy as jnp
from jax import lax
from jax.experimental import pallas as pl
from jax.experimental.pallas import tpu as pltpu
from jax.sharding import PartitionSpec as P

QUERY_HEADS = 64
KEY_VALUE_HEADS = 8
HEAD_SIZE = 128
GROUP_SIZE = QUERY_HEADS // KEY_VALUE_HEADS
BLK = 128
PROMPT_BLOCKS = 4
REPLY_BLOCKS = 2
MOST_BLOCKS = PROMPT_BLOCKS + REPLY_BLOCKS
CHIP_BLOCKS = 4
NEGATIVE_FILL = -1e30
EXP2_SCALE = 1.4426950408889634 * HEAD_SIZE ** (-0.5)
VMEM_LIMIT = 40 * 1024 * 1024
HEADS_AT_ONCE = 4


def attend(count, query, keys_now, values_now, out_ref):
    width = count * BLK
    row = lax.broadcasted_iota(jnp.int32, (BLK, BLK), 0)
    column = lax.broadcasted_iota(jnp.int32, (BLK, BLK), 1)
    causal = jnp.where(column <= row, 0.0, NEGATIVE_FILL)
    keys = keys_now[0:width, :]
    values = values_now[0:width, :]

    def scores(first):
        spans = [slice(h * HEAD_SIZE, (h + 1) * HEAD_SIZE) for h in range(first, first + HEADS_AT_ONCE)]
        stacked = jnp.concatenate([query[:, span] for span in spans], axis=0)
        score = lax.dot_general(stacked, keys, (((1,), (1,)), ((), ())), preferred_element_type=jnp.float32)
        return spans, score

    ahead = scores(0)
    for first in range(0, GROUP_SIZE, HEADS_AT_ONCE):
        spans, score = ahead
        if first + HEADS_AT_ONCE < GROUP_SIZE:
            ahead = scores(first + HEADS_AT_ONCE)
        parts = [score[:, i * BLK : (i + 1) * BLK] for i in range(count)]
        last = parts[-1].reshape(HEADS_AT_ONCE, BLK, BLK) + causal[None]
        parts[-1] = last.reshape(HEADS_AT_ONCE * BLK, BLK)
        peak = jnp.max(functools.reduce(jnp.maximum, parts), axis=1, keepdims=True) * EXP2_SCALE
        weight = [jnp.exp2(part * EXP2_SCALE - peak).astype(jnp.bfloat16) for part in parts]
        weight = weight[0] if count == 1 else jnp.concatenate(weight, axis=1)
        both = jnp.dot(weight, values, preferred_element_type=jnp.float32)
        result = (both[:, :HEAD_SIZE] / both[:, HEAD_SIZE:]).astype(out_ref.dtype)
        for h, span in enumerate(spans):
            out_ref[:, span] = result[h * BLK : (h + 1) * BLK]


def attention_kernel(slot_of, order, table_ref, query_ref, *refs):
    kv_refs = refs[:-8]
    out_ref, keys_now, values_now, ones_now, query_now, results, loaded, sent = refs[-8:]
    n_blocks, kv_heads, _, wide = results.shape
    chip = table_ref[3, 0] // CHIP_BLOCKS

    def query_copy(q_id, g):
        span = pl.ds(pl.multiple_of((table_ref[3, 1] * kv_heads + g) * wide, wide), wide)
        rows = pl.ds(q_id * BLK, BLK)
        return pltpu.make_async_copy(query_ref.at[rows, span], query_now.at[q_id, g], loaded.at[q_id, g])

    def result_copy(q_id, g):
        rows, span = pl.ds(q_id * BLK, BLK), pl.ds(pl.multiple_of(g * wide, wide), wide)
        return pltpu.make_async_copy(results.at[q_id, g], out_ref.at[rows, span], sent.at[q_id, g])

    for q_id in range(n_blocks):
        for g in range(kv_heads):
            query_copy(q_id, g).start()
    ones_now[:, HEAD_SIZE:] = jnp.ones((ones_now.shape[0], HEAD_SIZE), ones_now.dtype)
    for q_id in range(n_blocks):
        block = table_ref[3, 0] + q_id
        own = table_ref[0, block]
        first = table_ref[1, block]
        prompt = table_ref[2, block] - first
        count = prompt + block - own + 1
        for i in range(MOST_BLOCKS):
            which = jnp.where(i < prompt, first + i, own + i - prompt)
            slot = slot_of(table_ref, chip, which)
            to = slice(i * BLK, (i + 1) * BLK)
            if len(kv_refs) == 1:

                @pl.when(i < count)
                def _():
                    keys_now[to, :] = kv_refs[0][slot, 0:BLK, :]
                    values_now[to, :] = kv_refs[0][slot, BLK : 2 * BLK, :]

            else:
                choice = order(table_ref, slot)
                for j, kv_ref in enumerate(kv_refs):

                    @pl.when((i < count) & (choice == j))
                    def _():
                        keys_now[to, :] = kv_ref[0:BLK, :]
                        values_now[to, :] = kv_ref[BLK : 2 * BLK, :]

        for n in range(1, MOST_BLOCKS + 1):

            def one_head(g, carry):
                column = pl.multiple_of(g * HEAD_SIZE, HEAD_SIZE)
                width = n * BLK
                query_copy(q_id, g).wait()
                ones_now[0:width, :HEAD_SIZE] = values_now[0:width, pl.ds(column, HEAD_SIZE)]
                keys = keys_now.at[:, pl.ds(column, HEAD_SIZE)]
                attend(n, query_now.at[q_id, g], keys, ones_now, results.at[q_id, g])
                result_copy(q_id, g).start()
                return carry

            @pl.when(count == n)
            def _():
                lax.fori_loop(0, kv_heads, one_head, 0)

    for q_id in range(n_blocks):
        for g in range(kv_heads):
            result_copy(q_id, g).wait()


def attention(queries, cuts, kv, table, slot_of, order):
    rows, width = queries.shape[0], queries.shape[1] // cuts
    wide = GROUP_SIZE * HEAD_SIZE
    kv_heads = width // wide
    columns = kv[0].shape[-1]
    pieces = (rows // BLK, kv_heads)
    vmem = pl.BlockSpec(memory_space=pltpu.VMEM)
    smem = pl.BlockSpec(memory_space=pltpu.SMEM)
    kv = [pltpu.with_memory_space_constraint(array, pltpu.VMEM) for array in kv]
    return pl.pallas_call(
        functools.partial(attention_kernel, slot_of, order),
        in_specs=[smem, pl.BlockSpec(memory_space=pltpu.HBM)] + [vmem] * len(kv),
        out_specs=pl.BlockSpec(memory_space=pl.ANY),
        scratch_shapes=[
            pltpu.VMEM((MOST_BLOCKS * BLK, columns), jnp.bfloat16),
            pltpu.VMEM((MOST_BLOCKS * BLK, columns), jnp.bfloat16),
            pltpu.VMEM((MOST_BLOCKS * BLK, 2 * HEAD_SIZE), jnp.bfloat16),
            pltpu.VMEM(pieces + (BLK, wide), jnp.bfloat16),
            pltpu.VMEM(pieces + (BLK, wide), jnp.bfloat16),
            pltpu.SemaphoreType.DMA(pieces),
            pltpu.SemaphoreType.DMA(pieces),
        ],
        out_shape=jax.ShapeDtypeStruct((rows, width), jnp.bfloat16),
        compiler_params=pltpu.CompilerParams(vmem_limit_bytes=VMEM_LIMIT),
        name="attention",
    )(table, pltpu.with_memory_space_constraint(queries, pltpu.HBM), *kv)


def with_place(bounds, first_block, cut):
    place = jnp.where(jnp.arange(bounds.shape[1]) == 0, first_block, cut).astype(bounds.dtype)
    return jnp.concatenate([bounds, place[None]], 0)


def gathered_local(cuts, queries, keys, values, bounds):
    columns = KEY_VALUE_HEADS * HEAD_SIZE // cuts
    rows = keys.shape[0]
    both = jnp.stack([keys, values], 0).reshape(2, rows, cuts, columns)
    both = lax.all_to_all(both.transpose(2, 0, 1, 3), "cuts", 0, 0)
    both = lax.all_gather(both, "ctx", axis=0)
    both = both.transpose(2, 1, 0, 3, 4).reshape(2, -1, BLK, columns).transpose(1, 0, 2, 3)
    both = both.reshape(-1, 2 * BLK, columns)
    cut = lax.axis_index("cuts")
    table = with_place(bounds, lax.axis_index("ctx") * (queries.shape[0] // BLK), cut)
    return attention(queries, cuts, [both], table, lambda b, chip, which: which, None)


def crossing(table_ref, edge):
    own, first, last = table_ref[0, edge], table_ref[1, edge], table_ref[2, edge]
    reply = first < last
    return jnp.where(reply, first, own), jnp.where(reply, last, edge)


def crossing_block(table_ref, edge, residue):
    low, high = crossing(table_ref, edge)
    which = low + lax.rem(residue - lax.rem(low, 4) + 4, 4)
    return jnp.where(which < high, which, -1)


def tree_slot(table_ref, chip, which):
    edge = chip * CHIP_BLOCKS
    low, high = crossing(table_ref, edge)
    crosses = (which >= low) & (which < high)
    early = jnp.where(crosses, 4 + lax.rem(which, 4), 8)
    return jnp.where(which >= edge, which - edge, early)


def pick_kernel(rule, n_in, n_out, table_ref, *refs):
    ins, outs = refs[:n_in], refs[n_in : n_in + n_out]
    others = refs[n_in + n_out :]
    for out_ref, choice in zip(outs, rule(table_ref)):
        for i, in_ref in enumerate(ins):

            @pl.when(choice == i)
            def _():
                if others and i == n_in - 1:
                    copy = pltpu.make_async_copy(in_ref, out_ref, others[0])
                    copy.start()
                    copy.wait()
                else:
                    out_ref[...] = in_ref[...]


def pick(rule, n_out, table, *arrays, rare=None):
    vmem = pl.BlockSpec(memory_space=pltpu.VMEM)
    smem = pl.BlockSpec(memory_space=pltpu.SMEM)
    inputs = [pltpu.with_memory_space_constraint(array, pltpu.VMEM) for array in arrays]
    in_specs = [smem] + [vmem] * len(arrays)
    scratch = []
    if rare is not None:
        inputs.append(pltpu.with_memory_space_constraint(rare, pltpu.HBM))
        in_specs.append(pl.BlockSpec(memory_space=pltpu.HBM))
        scratch.append(pltpu.SemaphoreType.DMA)
    return pl.pallas_call(
        functools.partial(pick_kernel, rule, len(inputs), n_out),
        in_specs=in_specs,
        out_specs=[vmem] * n_out,
        out_shape=[pltpu.VMEM(arrays[0].shape, arrays[0].dtype)] * n_out,
        scratch_shapes=scratch,
        name="pick",
    )(table, *inputs)


def half(keys, values, cut):
    columns = keys.shape[1] // 2
    return jnp.concatenate([lax.dynamic_slice_in_dim(a, cut * columns, columns, 1) for a in (keys, values)], 0)


def where(*cases):
    value = cases[-1]
    for condition, choice in reversed(cases[:-1]):
        value = jnp.where(condition, choice, value)
    return value


def position(table_ref):
    ctx = table_ref[3, 0] // 2
    return ctx // 4, lax.rem(ctx, 4), lax.rem(ctx // 2, 2)


def rule_spread(table_ref):
    plane, _, _ = position(table_ref)
    cut = table_ref[3, 1]
    low, high = cut, 1 - cut
    return low, where((plane == 0, low), high), where((plane == 3, low), high)


def rule_middle(table_ref):
    plane, residue, x = position(table_ref)
    low, high, down, up, far = 0, 1, 2, 3, 4
    to_2 = crossing_block(table_ref, 16, residue)
    to_3 = crossing_block(table_ref, 24, residue)
    ahead = where(
        (plane == 1, jnp.where(to_2 < 4, up, low)),
        (plane == 2, where((to_3 < 12, low), (to_3 < 16, down), (to_3 < 20, far), up)),
        low,
    )
    lower = where((plane == 0, low), (plane == 1, down), (plane == 2, far), up)
    upper = where((plane == 0, down), (plane == 1, far), (plane == 2, up), high)
    kept = jnp.where(x == 0, lower, upper)
    sent = jnp.where(x == 0, upper, lower)
    return ahead, kept, sent, jnp.where(plane == 2, up, low)


def rule_last(table_ref):
    plane, residue, x = position(table_ref)
    low, down, up, kept, sent, crossed, rare = 0, 1, 2, 3, 4, 5, 6
    block = crossing_block(table_ref, plane * 8, residue)
    into_plane = where(
        (plane == 1, jnp.where(block < 4, up, low)),
        (plane == 2, where((block < 8, crossed), (block < 12, low), down)),
        (plane == 3, jnp.where((block >= 0) & (block < 8), rare, crossed)),
        low,
    )
    middle = crossing_block(table_ref, plane * 8 + 4, residue)
    into_half = jnp.where(middle >= plane * 8, jnp.where(x == 0, kept, sent), into_plane)
    return jnp.where(x == 0, into_plane, into_half), jnp.where(x == 0, into_half, into_plane)


def rule_before(table_ref):
    return (position(table_ref)[2],)


def tree_order(table_ref, slot):
    _, residue, _ = position(table_ref)
    flip = lax.rem(slot, 4) ^ residue
    index = 4 * lax.rem(flip, 2) + lax.rem(flip // 2, 2) + 2 * (slot // 4)
    return jnp.where(slot == 8, 9 - lax.rem(residue, 2), index)


def tree_local(queries, keys, values, bounds):
    cut = lax.axis_index("cuts")
    table = with_place(bounds, lax.axis_index("ctx") * 2, cut)
    own = half(keys, values, cut)
    other = lax.ppermute(half(keys, values, 1 - cut), "cuts", [(0, 1), (1, 0)])

    def move(array, planes):
        pairs = [(4 * a + r, 4 * b + r) for a, b in planes for r in range(4)]
        return lax.ppermute(array, "ctx", pairs)

    low, send_up, send_far = pick(rule_spread, 3, table, own, other)
    down = move(low, [(1, 0), (2, 1), (3, 2)])
    up = move(send_up, [(0, 1), (1, 2), (2, 3)])
    far = move(send_far, [(3, 1), (0, 2)])
    rare = lax.cond(crossing(bounds, 24)[0] < 8, lambda: move(low, [(1, 3)]), lambda: jnp.zeros_like(low))
    ahead, kept, sent, early = pick(rule_middle, 4, table, low, send_up, down, up, far, rare=rare)
    crossed = move(ahead, [(1, 2), (2, 3)])
    across = [(c, c ^ 2) for c in range(16)]
    beside = [(c, c ^ 1) for c in range(16)]
    home_x = lax.ppermute(sent, "ctx", across)
    before = lax.ppermute(early, "ctx", [(7, 5), (15, 9), (11, 13)])
    mine, forward = pick(rule_last, 2, table, low, down, up, kept, sent, crossed, rare=rare)
    far_x = lax.ppermute(forward, "ctx", across)
    (before,) = pick(rule_before, 1, table, before, sent)
    before_k = lax.ppermute(before, "ctx", [(c, c ^ 1) for c in range(1, 16, 2)])
    kv = [kept, home_x, mine, far_x]
    kv += [lax.ppermute(array, "ctx", beside) for array in kv]
    kv += [before, before_k]
    return attention(queries, 2, kv, table, tree_slot, tree_order)


def solution(mesh):
    cuts, ctx = mesh.shape["cuts"], mesh.shape["ctx"]
    in_specs = (P("ctx", None), P(("cuts", "ctx"), None), P(("cuts", "ctx"), None), P())
    out_specs = P("ctx", "cuts")
    general = functools.partial(gathered_local, cuts)

    def run(queries, keys, values, bounds):
        one_block_each = keys.shape[0] == cuts * ctx * BLK
        local = tree_local if (cuts, ctx) == (2, 16) and one_block_each else general
        mapped = jax.shard_map(local, mesh=mesh, in_specs=in_specs, out_specs=out_specs, check_vma=False)
        return mapped(queries, keys, values, bounds)

    return run
```

```python
import functools

import jax
import jax.numpy as jnp
from jax import lax
from jax.experimental import pallas as pl
from jax.experimental.pallas import tpu as pltpu
from jax.sharding import PartitionSpec as P

QUERY_HEADS = 64
KEY_VALUE_HEADS = 8
HEAD_SIZE = 128
GROUP_SIZE = QUERY_HEADS // KEY_VALUE_HEADS
BLK = 128
PROMPT_BLOCKS = 4
REPLY_BLOCKS = 2
MOST_BLOCKS = PROMPT_BLOCKS + REPLY_BLOCKS
CHIP_BLOCKS = 4
NEGATIVE_FILL = -1e30
EXP2_SCALE = 1.4426950408889634 * HEAD_SIZE ** (-0.5)
VMEM_LIMIT = 40 * 1024 * 1024
HEADS_AT_ONCE = 2


def attend(count, query, keys_now, values_now, out_ref):
    width = count * BLK
    row = lax.broadcasted_iota(jnp.int32, (BLK, BLK), 0)
    column = lax.broadcasted_iota(jnp.int32, (BLK, BLK), 1)
    causal = jnp.where(column <= row, 0.0, NEGATIVE_FILL)
    keys = keys_now[0:width, :]
    values = values_now[0:width, :]

    def scores(first):
        spans = [slice(h * HEAD_SIZE, (h + 1) * HEAD_SIZE) for h in range(first, first + HEADS_AT_ONCE)]
        stacked = jnp.concatenate([query[:, span] for span in spans], axis=0)
        score = lax.dot_general(stacked, keys, (((1,), (1,)), ((), ())), preferred_element_type=jnp.float32)
        return spans, score

    ahead = scores(0)
    waiting = None
    for first in range(0, GROUP_SIZE, HEADS_AT_ONCE):
        spans, score = ahead
        if first + HEADS_AT_ONCE < GROUP_SIZE:
            ahead = scores(first + HEADS_AT_ONCE)
        parts = [score[:, i * BLK : (i + 1) * BLK] for i in range(count)]
        last = parts[-1].reshape(HEADS_AT_ONCE, BLK, BLK) + causal[None]
        parts[-1] = last.reshape(HEADS_AT_ONCE * BLK, BLK)
        peak = jnp.max(functools.reduce(jnp.maximum, parts), axis=1, keepdims=True)
        weight = [jnp.exp2((part - peak) * EXP2_SCALE).astype(jnp.bfloat16) for part in parts]
        weight = weight[0] if count == 1 else jnp.concatenate(weight, axis=1)
        if waiting is not None:
            finish_heads(values, out_ref, *waiting)
        waiting = spans, weight
    finish_heads(values, out_ref, *waiting)


def finish_heads(values, out_ref, spans, weight):
    both = jnp.dot(weight, values, preferred_element_type=jnp.float32)
    result = (both[:, :HEAD_SIZE] / both[:, HEAD_SIZE:]).astype(out_ref.dtype)
    for h, span in enumerate(spans):
        out_ref[:, span] = result[h * BLK : (h + 1) * BLK]


def attention_kernel(slot_of, order, table_ref, query_ref, *refs):
    kv_refs = refs[:-8]
    out_ref, keys_now, values_now, ones_now, query_now, results, loaded, sent = refs[-8:]
    n_blocks, kv_heads, _, wide = results.shape
    chip = table_ref[3, 0] // CHIP_BLOCKS

    def query_copy(q_id, g):
        span = pl.ds(pl.multiple_of((table_ref[3, 1] * kv_heads + g) * wide, wide), wide)
        rows = pl.ds(q_id * BLK, BLK)
        return pltpu.make_async_copy(query_ref.at[rows, span], query_now.at[q_id, g], loaded.at[q_id, g])

    def result_copy(q_id, g):
        rows, span = pl.ds(q_id * BLK, BLK), pl.ds(pl.multiple_of(g * wide, wide), wide)
        return pltpu.make_async_copy(results.at[q_id, g], out_ref.at[rows, span], sent.at[q_id, g])

    for q_id in range(n_blocks):
        for g in range(kv_heads):
            query_copy(q_id, g).start()
    ones_now[:, HEAD_SIZE:] = jnp.ones((ones_now.shape[0], HEAD_SIZE), ones_now.dtype)
    for q_id in range(n_blocks):
        block = table_ref[3, 0] + q_id
        own = table_ref[0, block]
        first = table_ref[1, block]
        prompt = table_ref[2, block] - first
        count = prompt + block - own + 1
        for i in range(MOST_BLOCKS):
            which = jnp.where(i < prompt, first + i, own + i - prompt)
            slot = slot_of(table_ref, chip, which)
            to = slice(i * BLK, (i + 1) * BLK)
            if len(kv_refs) == 1:

                @pl.when(i < count)
                def _():
                    keys_now[to, :] = kv_refs[0][slot, 0:BLK, :]
                    values_now[to, :] = kv_refs[0][slot, BLK : 2 * BLK, :]

            else:
                choice = order(table_ref, slot)
                for j, kv_ref in enumerate(kv_refs):

                    @pl.when((i < count) & (choice == j))
                    def _():
                        keys_now[to, :] = kv_ref[0:BLK, :]
                        values_now[to, :] = kv_ref[BLK : 2 * BLK, :]

        for n in range(1, MOST_BLOCKS + 1):

            def one_head(g, carry):
                column = pl.multiple_of(g * HEAD_SIZE, HEAD_SIZE)
                width = n * BLK
                query_copy(q_id, g).wait()
                ones_now[0:width, :HEAD_SIZE] = values_now[0:width, pl.ds(column, HEAD_SIZE)]
                keys = keys_now.at[:, pl.ds(column, HEAD_SIZE)]
                attend(n, query_now.at[q_id, g], keys, ones_now, results.at[q_id, g])
                result_copy(q_id, g).start()
                return carry

            @pl.when(count == n)
            def _():
                lax.fori_loop(0, kv_heads, one_head, 0)

    for q_id in range(n_blocks):
        for g in range(kv_heads):
            result_copy(q_id, g).wait()


def attention(queries, cuts, kv, table, slot_of, order):
    rows, width = queries.shape[0], queries.shape[1] // cuts
    wide = GROUP_SIZE * HEAD_SIZE
    kv_heads = width // wide
    columns = kv[0].shape[-1]
    pieces = (rows // BLK, kv_heads)
    vmem = pl.BlockSpec(memory_space=pltpu.VMEM)
    smem = pl.BlockSpec(memory_space=pltpu.SMEM)
    kv = [pltpu.with_memory_space_constraint(array, pltpu.VMEM) for array in kv]
    return pl.pallas_call(
        functools.partial(attention_kernel, slot_of, order),
        in_specs=[smem, pl.BlockSpec(memory_space=pltpu.HBM)] + [vmem] * len(kv),
        out_specs=pl.BlockSpec(memory_space=pl.ANY),
        scratch_shapes=[
            pltpu.VMEM((MOST_BLOCKS * BLK, columns), jnp.bfloat16),
            pltpu.VMEM((MOST_BLOCKS * BLK, columns), jnp.bfloat16),
            pltpu.VMEM((MOST_BLOCKS * BLK, 2 * HEAD_SIZE), jnp.bfloat16),
            pltpu.VMEM(pieces + (BLK, wide), jnp.bfloat16),
            pltpu.VMEM(pieces + (BLK, wide), jnp.bfloat16),
            pltpu.SemaphoreType.DMA(pieces),
            pltpu.SemaphoreType.DMA(pieces),
        ],
        out_shape=jax.ShapeDtypeStruct((rows, width), jnp.bfloat16),
        compiler_params=pltpu.CompilerParams(vmem_limit_bytes=VMEM_LIMIT),
        name="attention",
    )(table, pltpu.with_memory_space_constraint(queries, pltpu.HBM), *kv)


def with_place(bounds, first_block, cut):
    place = jnp.where(jnp.arange(bounds.shape[1]) == 0, first_block, cut).astype(bounds.dtype)
    return jnp.concatenate([bounds, place[None]], 0)


def gathered_local(cuts, queries, keys, values, bounds):
    columns = KEY_VALUE_HEADS * HEAD_SIZE // cuts
    rows = keys.shape[0]
    both = jnp.stack([keys, values], 0).reshape(2, rows, cuts, columns)
    both = lax.all_to_all(both.transpose(2, 0, 1, 3), "cuts", 0, 0)
    both = lax.all_gather(both, "ctx", axis=0)
    both = both.transpose(2, 1, 0, 3, 4).reshape(2, -1, BLK, columns).transpose(1, 0, 2, 3)
    both = both.reshape(-1, 2 * BLK, columns)
    cut = lax.axis_index("cuts")
    table = with_place(bounds, lax.axis_index("ctx") * (queries.shape[0] // BLK), cut)
    return attention(queries, cuts, [both], table, lambda b, chip, which: which, None)


def crossing(table_ref, edge):
    own, first, last = table_ref[0, edge], table_ref[1, edge], table_ref[2, edge]
    reply = first < last
    return jnp.where(reply, first, own), jnp.where(reply, last, edge)


def crossing_block(table_ref, edge, residue):
    low, high = crossing(table_ref, edge)
    which = low + lax.rem(residue - lax.rem(low, 4) + 4, 4)
    return jnp.where(which < high, which, -1)


def tree_slot(table_ref, chip, which):
    edge = chip * CHIP_BLOCKS
    low, high = crossing(table_ref, edge)
    crosses = (which >= low) & (which < high)
    early = jnp.where(crosses, 4 + lax.rem(which, 4), 8)
    return jnp.where(which >= edge, which - edge, early)


def pick_kernel(rule, n_in, n_out, table_ref, *refs):
    ins, outs = refs[:n_in], refs[n_in : n_in + n_out]
    others = refs[n_in + n_out :]
    for out_ref, choice in zip(outs, rule(table_ref)):
        for i, in_ref in enumerate(ins):

            @pl.when(choice == i)
            def _():
                if others and i == n_in - 1:
                    copy = pltpu.make_async_copy(in_ref, out_ref, others[0])
                    copy.start()
                    copy.wait()
                else:
                    out_ref[...] = in_ref[...]


def pick(rule, n_out, table, *arrays, rare=None):
    vmem = pl.BlockSpec(memory_space=pltpu.VMEM)
    smem = pl.BlockSpec(memory_space=pltpu.SMEM)
    inputs = [pltpu.with_memory_space_constraint(array, pltpu.VMEM) for array in arrays]
    in_specs = [smem] + [vmem] * len(arrays)
    scratch = []
    if rare is not None:
        inputs.append(pltpu.with_memory_space_constraint(rare, pltpu.HBM))
        in_specs.append(pl.BlockSpec(memory_space=pltpu.HBM))
        scratch.append(pltpu.SemaphoreType.DMA)
    return pl.pallas_call(
        functools.partial(pick_kernel, rule, len(inputs), n_out),
        in_specs=in_specs,
        out_specs=[vmem] * n_out,
        out_shape=[pltpu.VMEM(arrays[0].shape, arrays[0].dtype)] * n_out,
        scratch_shapes=scratch,
        name="pick",
    )(table, *inputs)


def half(keys, values, cut):
    columns = keys.shape[1] // 2
    return jnp.concatenate([lax.dynamic_slice_in_dim(a, cut * columns, columns, 1) for a in (keys, values)], 0)


def where(*cases):
    value = cases[-1]
    for condition, choice in reversed(cases[:-1]):
        value = jnp.where(condition, choice, value)
    return value


def position(table_ref):
    ctx = table_ref[3, 0] // 2
    return ctx // 4, lax.rem(ctx, 4), lax.rem(ctx // 2, 2)


def rule_spread(table_ref):
    plane, _, _ = position(table_ref)
    cut = table_ref[3, 1]
    low, high = cut, 1 - cut
    return low, where((plane == 0, low), high), where((plane == 3, low), high)


def rule_middle(table_ref):
    plane, residue, x = position(table_ref)
    low, high, down, up, far = 0, 1, 2, 3, 4
    to_2 = crossing_block(table_ref, 16, residue)
    to_3 = crossing_block(table_ref, 24, residue)
    ahead = where(
        (plane == 1, jnp.where(to_2 < 4, up, low)),
        (plane == 2, where((to_3 < 12, low), (to_3 < 16, down), (to_3 < 20, far), up)),
        low,
    )
    lower = where((plane == 0, low), (plane == 1, down), (plane == 2, far), up)
    upper = where((plane == 0, down), (plane == 1, far), (plane == 2, up), high)
    kept = jnp.where(x == 0, lower, upper)
    sent = jnp.where(x == 0, upper, lower)
    return ahead, kept, sent, jnp.where(plane == 2, up, low)


def rule_last(table_ref):
    plane, residue, x = position(table_ref)
    low, down, up, kept, sent, crossed, rare = 0, 1, 2, 3, 4, 5, 6
    block = crossing_block(table_ref, plane * 8, residue)
    into_plane = where(
        (plane == 1, jnp.where(block < 4, up, low)),
        (plane == 2, where((block < 8, crossed), (block < 12, low), down)),
        (plane == 3, jnp.where((block >= 0) & (block < 8), rare, crossed)),
        low,
    )
    middle = crossing_block(table_ref, plane * 8 + 4, residue)
    into_half = jnp.where(middle >= plane * 8, jnp.where(x == 0, kept, sent), into_plane)
    return jnp.where(x == 0, into_plane, into_half), jnp.where(x == 0, into_half, into_plane)


def rule_before(table_ref):
    return (position(table_ref)[2],)


def tree_order(table_ref, slot):
    _, residue, _ = position(table_ref)
    flip = lax.rem(slot, 4) ^ residue
    index = 4 * lax.rem(flip, 2) + lax.rem(flip // 2, 2) + 2 * (slot // 4)
    return jnp.where(slot == 8, 9 - lax.rem(residue, 2), index)


def tree_local(queries, keys, values, bounds):
    cut = lax.axis_index("cuts")
    table = with_place(bounds, lax.axis_index("ctx") * 2, cut)
    own = half(keys, values, cut)
    other = lax.ppermute(half(keys, values, 1 - cut), "cuts", [(0, 1), (1, 0)])

    def move(array, planes):
        pairs = [(4 * a + r, 4 * b + r) for a, b in planes for r in range(4)]
        return lax.ppermute(array, "ctx", pairs)

    low, send_up, send_far = pick(rule_spread, 3, table, own, other)
    down = move(low, [(1, 0), (2, 1), (3, 2)])
    up = move(send_up, [(0, 1), (1, 2), (2, 3)])
    far = move(send_far, [(3, 1), (0, 2)])
    rare = lax.cond(crossing(bounds, 24)[0] < 8, lambda: move(low, [(1, 3)]), lambda: jnp.zeros_like(low))
    ahead, kept, sent, early = pick(rule_middle, 4, table, low, send_up, down, up, far, rare=rare)
    crossed = move(ahead, [(1, 2), (2, 3)])
    across = [(c, c ^ 2) for c in range(16)]
    beside = [(c, c ^ 1) for c in range(16)]
    home_x = lax.ppermute(sent, "ctx", across)
    before = lax.ppermute(early, "ctx", [(7, 5), (15, 9), (11, 13)])
    mine, forward = pick(rule_last, 2, table, low, down, up, kept, sent, crossed, rare=rare)
    far_x = lax.ppermute(forward, "ctx", across)
    (before,) = pick(rule_before, 1, table, before, sent)
    before_k = lax.ppermute(before, "ctx", [(c, c ^ 1) for c in range(1, 16, 2)])
    kv = [kept, home_x, mine, far_x]
    kv += [lax.ppermute(array, "ctx", beside) for array in kv]
    kv += [before, before_k]
    return attention(queries, 2, kv, table, tree_slot, tree_order)


def solution(mesh):
    cuts, ctx = mesh.shape["cuts"], mesh.shape["ctx"]
    in_specs = (P("ctx", None), P(("cuts", "ctx"), None), P(("cuts", "ctx"), None), P())
    out_specs = P("ctx", "cuts")
    general = functools.partial(gathered_local, cuts)

    def run(queries, keys, values, bounds):
        one_block_each = keys.shape[0] == cuts * ctx * BLK
        local = tree_local if (cuts, ctx) == (2, 16) and one_block_each else general
        mapped = jax.shard_map(local, mesh=mesh, in_specs=in_specs, out_specs=out_specs, check_vma=False)
        return mapped(queries, keys, values, bounds)

    return run
```
